32 devices in a mesh: grp: 2 (over x), lon: 16 (over z, y, core).
Axes of the slice: x: 2, y: 2, z: 4, core: 2. Of those that a mesh axis runs over, the one named last changes fastest.
Arguments:
- latent: bfloat16 [128, 256, 1024], P('grp', 'lon'), parts along dimension 0, may hold values from -6 to 6
- filters: bfloat16 [9, 128, 256], replicated, may hold values from -0.375 to 0.375
- quadrature: float32 [64], replicated, may hold values from 0.3 to 3
- basis_values: bfloat16 [128, 8, 64, 32], replicated, may hold values from -0.375 to 0.375
- source_row: int32 [128, 8], replicated, may hold values from 0 to 63, as said below
- offset: int32 [128, 8], replicated, may hold values from -1 to 1
- basis_index: int32 [128, 8], replicated, may hold values from 0 to 8
- across_pole: int32 [128, 8], replicated, may hold values from 0 to 1, as said below
Outputs:
- upsampled: bfloat16 [256, 2048, 128], P('grp', 'lon'), parts along dimension 0
The draws below stay inside these ranges and needn't reach their ends.
There are 2 independent parts, one for each index of `grp`. The reference program is written for one: setup_inputs(seed, part) draws one part's arguments, and reference() takes and returns one part's arrays. A program takes and returns all parts, laid end to end along the dimension named above; an argument that names none is the same for every part. Nothing has to cross between parts.
Inputs may be any that keep to these rules, and one draw needn't show every extreme that they name: Where across_pole is 1, source_row is under 16; elsewhere it lies within one of h / 2 for output row h (clipped to the rows). across_pole is 1 only in the first 32 output rows.
All inputs are finite; a program needn't handle non-finite values.
Results may differ from the reference program's by a relative error of at most 0.0065.
Values may be sent and summed in bfloat16 or wider, within the bound.
A program may use at most 256 MiB of HBM per device.

```python
import math
import jax
import jax.numpy as jnp
from jax import lax

CH_IN = 256
CH_OUT = 128
BASES = 9
ENTRIES = 8
LAT_IN = 64
LAT_OUT = 128
POLE_ROWS = 32
POLE_SRC = 16
LON_IN = 1024


def pole_pattern(key):
    row_ids = jnp.arange(LAT_OUT, dtype=jnp.int32)[:, None]
    columns = jnp.arange(ENTRIES, dtype=jnp.int32)[None, :]
    flags = jax.random.randint(jax.random.fold_in(key, 101), (LAT_OUT, ENTRIES), 0, 2)
    flags = jnp.where(row_ids < POLE_ROWS, flags, 0)
    flags = jnp.where(columns == 0, 0, flags)
    flags = jnp.where((row_ids == 0) & (columns == ENTRIES - 1), 1, flags)
    deltas = jax.random.randint(jax.random.fold_in(key, 102), (LAT_OUT, ENTRIES), -1, 2)
    deltas = jnp.where(columns == 0, 0, deltas)
    near_rows = jnp.clip(row_ids // 2 + deltas, 0, LAT_IN - 1)
    far_rows = jax.random.randint(jax.random.fold_in(key, 103), (LAT_OUT, ENTRIES), 0, POLE_SRC)
    return (flags.astype(jnp.int32), jnp.where(flags == 1, far_rows, near_rows).astype(jnp.int32))


def draw_across_pole(key, part):
    return pole_pattern(key)[0]


def draw_source_row(key, part):
    return pole_pattern(key)[1]


def touch_ends(array, stream_key, least, high):
    index_at = [jax.random.randint(jax.random.fold_in(stream_key, axis), (), 0, length) for axis, length in enumerate(array.shape)]
    longest = array.shape.index(max(array.shape))
    next_to = index_at[:longest] + [(index_at[longest] + 1) % array.shape[longest]] + index_at[longest + 1:]
    return array.at[tuple(index_at)].set(least).at[tuple(next_to)].set(high)


def shard_levels(key, extent, cuts, low, high):
    def one(axis_at, shards_of):
        heights = jax.random.uniform(jax.random.fold_in(jax.random.fold_in(key, 6), axis_at), (shards_of,), jnp.float32, low / len(cuts), high / len(cuts))
        return jnp.repeat(jnp.exp(heights), extent[axis_at] // shards_of).reshape((-1,) + (1,) * (len(extent) - axis_at - 1))

    level = one(*cuts[0])
    for cut in cuts[1:]:
        level = level * one(*cut)
    return level


def noise(stream_key, shape, width, most, pieces=(), kind=jnp.bfloat16):
    values = width * jax.random.normal(stream_key, shape, jnp.float32)
    if pieces:
        values = values * shard_levels(stream_key, shape, pieces, -0.22, 0.18)
    return jnp.clip(values, -most, most).astype(kind)


def setup_inputs(seed: int = 0, part: int = 0) -> dict:
    streams_of = jax.random.split(jax.random.key(seed), 9)
    part_keys = jax.random.split(jax.random.fold_in(streams_of[8], part), 9)
    latent = noise(part_keys[0], (LAT_IN, CH_IN, LON_IN), 1.0, 6.0, ((1, 16),))
    filters = noise(streams_of[1], (BASES, CH_OUT, CH_IN), CH_IN ** -0.5, 0.375)
    quadrature = jnp.clip(jnp.exp(jax.random.uniform(streams_of[2], (LAT_IN,), jnp.float32, math.log(0.3), math.log(3.0))), 0.3, 3.0)
    basis_values = noise(streams_of[3], (LAT_OUT, ENTRIES, 64, 32), (ENTRIES * 32) ** -0.5, 0.375)
    source_row = draw_source_row(jax.random.fold_in(streams_of[8], 71), part)
    offset = touch_ends(jax.random.randint(streams_of[5], (LAT_OUT, ENTRIES), -1, 2), jax.random.fold_in(streams_of[5], 1), -1, 1).astype(jnp.int32)
    basis_index = touch_ends(jax.random.randint(streams_of[6], (LAT_OUT, ENTRIES), 0, BASES), jax.random.fold_in(streams_of[6], 1), 0, BASES - 1).astype(jnp.int32)
    across_pole = draw_across_pole(jax.random.fold_in(streams_of[8], 71), part)
    return {"latent": latent, "filters": filters, "quadrature": quadrature, "basis_values": basis_values, "source_row": source_row, "offset": offset, "basis_index": basis_index, "across_pole": across_pole}


def reference(latent, filters, quadrature, basis_values, source_row, offset, basis_index, across_pole):
    filt32 = filters.astype(jnp.float32)

    def mix_row(item):
        plane_row, weight = item
        mixed = jnp.einsum("kci,iw->kwc", filt32, plane_row.astype(jnp.float32), precision=lax.Precision.HIGHEST)
        return (mixed * weight).astype(jnp.bfloat16)

    mixed_basis = lax.map(mix_row, (latent, quadrature))
    in_blocks = LON_IN // 32
    half_blocks = in_blocks // 2
    blocked = mixed_basis.reshape(LAT_IN, BASES, in_blocks, 32, CH_OUT)

    def out_row(item):
        values, sources, offsets, kind_row, pole_row = item
        summed = jnp.zeros((in_blocks, 64, CH_OUT), jnp.float32)
        for j in range(ENTRIES):
            plane_row = blocked[sources[j], kind_row[j]]
            rotation = offsets[j] - pole_row[j] * half_blocks
            block_ids = ((jnp.arange(in_blocks, dtype=jnp.int32) - rotation) % in_blocks).astype(jnp.int32)
            plane_row = jnp.take(plane_row, block_ids, axis=0)
            summed = summed + jnp.einsum("nvc,uv->nuc", plane_row.astype(jnp.float32), values[j].astype(jnp.float32), precision=lax.Precision.HIGHEST)
        return summed.reshape(in_blocks * 64, CH_OUT).astype(jnp.bfloat16)

    return lax.map(out_row, (basis_values, source_row, offset, basis_index, across_pole))
```

```python
import functools

import jax
import jax.numpy as jnp
from jax import lax
from jax.experimental import pallas as pl
from jax.experimental.pallas import tpu as pltpu
from jax.sharding import PartitionSpec as P

BLOCK = 32
FINE = 64
MIX_ROWS = 4
OUT_ROWS = 8


def from_behind(block, axis, distance):
    devices = range(lax.axis_size(axis))
    route = [((i - distance) % len(devices), i) for i in devices]
    return lax.ppermute(block, axis, route)


def compute(mix_steps, bases, entries, rows_ref, starts_ref, quad_ref, ext_ref, filt_ref, values_ref, out_ref, mixed):
    step = pl.program_id(0)
    channels = out_ref.shape[2]

    @pl.when(step < mix_steps)
    def _():
        for r in range(MIX_ROWS):
            row = step * MIX_ROWS + r
            product = lax.dot_general(
                ext_ref[r], filt_ref[...], (((0,), (0,)), ((), ())), preferred_element_type=jnp.float32
            )
            product = (product * quad_ref[row]).astype(jnp.bfloat16)
            for k in range(bases):
                mixed[row * bases + k] = product[:, k * channels : (k + 1) * channels]

    @pl.when(step >= mix_steps)
    def _():
        for g in range(OUT_ROWS):
            h = (step - mix_steps) * OUT_ROWS + g
            parts = []
            for j in range(entries):
                e = h * entries + j
                start = pl.multiple_of(starts_ref[e], BLOCK)
                parts.append(mixed[rows_ref[e], pl.ds(start, 2 * BLOCK), :])
            first = jnp.concatenate([p[:BLOCK] for p in parts], axis=0)
            second = jnp.concatenate([p[BLOCK:] for p in parts], axis=0)
            terms = jnp.concatenate([first, second], axis=1)
            values = jnp.concatenate([values_ref[g, j] for j in range(entries)], axis=1)
            total = jnp.dot(values, terms, preferred_element_type=jnp.float32)
            total = total.astype(jnp.bfloat16)
            out_ref[g, :FINE] = total[:, :channels]
            out_ref[g, FINE:] = total[:, channels:]


def on_device(
    latent, filters, quadrature, basis_values, source_row, offset, basis_index, across_pole
):
    source_total = latent.shape[0]
    row_total, entries = source_row.shape
    bases, channels, deep = filters.shape
    pole_source = source_total // 4
    half = latent.shape[2] // 2
    turned = jnp.roll(latent[:pole_source], half, axis=2)
    stacked = jnp.concatenate([latent, turned], axis=0)
    tile = lax.all_to_all(stacked, "lon", split_axis=2, concat_axis=1, tiled=True)
    left = from_behind(tile[:, :, BLOCK:], "lon", 1)
    right = from_behind(tile[:, :, :BLOCK], "lon", -1)
    ext = jnp.concatenate([left, tile, right], axis=2)
    rows = ((source_row + source_total * across_pole) * bases + basis_index).reshape(-1)
    starts = ((1 - offset) * BLOCK).reshape(-1)
    quad = jnp.concatenate([quadrature, quadrature[:pole_source]])
    filt = filters.reshape(bases * channels, deep).T
    all_rows = source_total + pole_source
    mix_steps = all_rows // MIX_ROWS
    out_steps = row_total // OUT_ROWS
    smem = pl.BlockSpec(memory_space=pltpu.SMEM)
    width = ext.shape[2]
    last = lambda i: jnp.maximum(i - mix_steps, 0)
    return pl.pallas_call(
        functools.partial(compute, mix_steps, bases, entries),
        grid=(mix_steps + out_steps,),
        out_shape=jax.ShapeDtypeStruct((row_total, 2 * FINE, channels), jnp.bfloat16),
        in_specs=[
            smem,
            smem,
            smem,
            pl.BlockSpec((MIX_ROWS, deep, width), lambda i: (jnp.minimum(i, mix_steps - 1), 0, 0)),
            pl.BlockSpec((deep, bases * channels), lambda i: (0, 0)),
            pl.BlockSpec((OUT_ROWS, entries, FINE, BLOCK), lambda i: (last(i), 0, 0, 0)),
        ],
        out_specs=pl.BlockSpec((OUT_ROWS, 2 * FINE, channels), lambda i: (last(i), 0, 0)),
        scratch_shapes=[pltpu.VMEM((all_rows * bases, width, channels), jnp.bfloat16)],
        compiler_params=pltpu.CompilerParams(vmem_limit_bytes=48 * 2**20),
    )(rows, starts, quad, ext, filt, basis_values)


def solution(mesh):
    in_specs = (P("grp", "lon", None), P(), P(), P(), P(), P(), P(), P())
    out_specs = P("grp", "lon", None)
    return jax.shard_map(
        on_device, mesh=mesh, in_specs=in_specs, out_specs=out_specs, check_vma=False
    )
```

```python
import functools

import jax
import jax.numpy as jnp
from jax import lax
from jax.experimental import pallas as pl
from jax.experimental.pallas import tpu as pltpu
from jax.sharding import PartitionSpec as P

BLOCK = 32
FINE = 64
MIX_ROWS = 4
OUT_ROWS = 8
MESH = pl.DeviceIdType.MESH


def from_behind(block, axis, distance):
    devices = range(lax.axis_size(axis))
    route = [((i - distance) % len(devices), i) for i in devices]
    return lax.ppermute(block, axis, route)


def compute(mix_steps, bases, entries, rows_ref, starts_ref, quad_ref, ext_ref, filt_ref, values_ref, out_ref, mixed):
    step = pl.program_id(0)
    channels = out_ref.shape[2]

    @pl.when(step < mix_steps)
    def _():
        for r in range(MIX_ROWS):
            row = step * MIX_ROWS + r
            product = lax.dot_general(
                ext_ref[r], filt_ref[...], (((0,), (0,)), ((), ())), preferred_element_type=jnp.float32
            )
            product = (product * quad_ref[row]).astype(jnp.bfloat16)
            for k in range(bases):
                mixed[row * bases + k] = product[:, k * channels : (k + 1) * channels]

    @pl.when(step >= mix_steps)
    def _():
        for g in range(OUT_ROWS):
            h = (step - mix_steps) * OUT_ROWS + g
            parts = []
            for j in range(entries):
                e = h * entries + j
                start = pl.multiple_of(starts_ref[e], BLOCK)
                parts.append(mixed[rows_ref[e], pl.ds(start, 2 * BLOCK), :])
            first = jnp.concatenate([p[:BLOCK] for p in parts], axis=0)
            second = jnp.concatenate([p[BLOCK:] for p in parts], axis=0)
            terms = jnp.concatenate([first, second], axis=1)
            values = jnp.concatenate([values_ref[g, j] for j in range(entries)], axis=1)
            total = jnp.dot(values, terms, preferred_element_type=jnp.float32)
            total = total.astype(jnp.bfloat16)
            out_ref[g, :FINE] = total[:, :channels]
            out_ref[g, FINE:] = total[:, channels:]


def on_device(
    latent, filters, quadrature, basis_values, source_row, offset, basis_index, across_pole
):
    source_total = latent.shape[0]
    row_total, entries = source_row.shape
    bases, channels, deep = filters.shape
    pole_source = source_total // 4
    half = latent.shape[2] // 2
    turned = jnp.roll(latent[:pole_source], half, axis=2)
    stacked = jnp.concatenate([latent, turned], axis=0)
    tile = lax.all_to_all(stacked, "lon", split_axis=2, concat_axis=1, tiled=True)
    left = from_behind(tile[:, :, BLOCK:], "lon", 1)
    right = from_behind(tile[:, :, :BLOCK], "lon", -1)
    ext = jnp.concatenate([left, tile, right], axis=2)
    rows = ((source_row + source_total * across_pole) * bases + basis_index).reshape(-1)
    starts = ((1 - offset) * BLOCK).reshape(-1)
    quad = jnp.concatenate([quadrature, quadrature[:pole_source]])
    filt = filters.reshape(bases * channels, deep).T
    all_rows = source_total + pole_source
    mix_steps = all_rows // MIX_ROWS
    out_steps = row_total // OUT_ROWS
    smem = pl.BlockSpec(memory_space=pltpu.SMEM)
    width = ext.shape[2]
    last = lambda i: jnp.maximum(i - mix_steps, 0)
    return pl.pallas_call(
        functools.partial(compute, mix_steps, bases, entries),
        grid=(mix_steps + out_steps,),
        out_shape=jax.ShapeDtypeStruct((row_total, 2 * FINE, channels), jnp.bfloat16),
        in_specs=[
            smem,
            smem,
            smem,
            pl.BlockSpec((MIX_ROWS, deep, width), lambda i: (jnp.minimum(i, mix_steps - 1), 0, 0)),
            pl.BlockSpec((deep, bases * channels), lambda i: (0, 0)),
            pl.BlockSpec((OUT_ROWS, entries, FINE, BLOCK), lambda i: (last(i), 0, 0, 0)),
        ],
        out_specs=pl.BlockSpec((OUT_ROWS, 2 * FINE, channels), lambda i: (last(i), 0, 0)),
        scratch_shapes=[pltpu.VMEM((all_rows * bases, width, channels), jnp.bfloat16)],
        compiler_params=pltpu.CompilerParams(vmem_limit_bytes=48 * 2**20),
    )(rows, starts, quad, ext, filt, basis_values)


def exchange(axis, lat_ref, recv, from_left, from_right, pack, go_right, go_left, sends, recvs, halo_sends, halo_recvs):
    n = lax.axis_size(axis)
    me = lax.axis_index(axis)
    right, left = lax.rem(me + 1, n), lax.rem(me + n - 1, n)
    pairs = lat_ref.shape[0] // 8
    sections = lat_ref.shape[0] // (2 * pairs) + 1
    quads = pairs // 2
    deep = go_right.shape[1]
    channels = lat_ref.shape[1]

    barrier = pltpu.get_barrier_semaphore()

    @pl.loop(1, n)
    def _(distance):
        peer = lax.rem(me + distance, n)
        pl.semaphore_signal(barrier, inc=1, device_id={axis: peer}, device_id_type=MESH)

    pl.semaphore_wait(barrier, n - 1)

    def source(section, target):
        if section == 1:
            return pack.at[lax.rem(target + n // 2, n), pl.ds(0, pairs)]
        return pack.at[target, pl.ds(max(section - 1, 0) * pairs, pairs)]

    def piece(section, target, sender, peer):
        return pltpu.make_async_remote_copy(
            src_ref=source(section, target),
            dst_ref=recv.at[pl.ds(section * pairs, pairs), sender],
            send_sem=sends.at[section, target],
            recv_sem=recvs.at[section, sender],
            device_id={axis: peer},
            device_id_type=MESH,
        )

    def halo(section, way):
        held, landed, peer = (go_right, from_left, right) if way == 0 else (go_left, from_right, left)
        part = pl.ds(section * quads, quads)
        return pltpu.make_async_remote_copy(
            src_ref=held.at[part],
            dst_ref=landed.at[part],
            send_sem=halo_sends.at[section, way],
            recv_sem=halo_recvs.at[section, way],
            device_id={axis: peer},
            device_id_type=MESH,
        )

    for section in range(sections):
        if section != 1:
            first = max(section - 1, 0) * pairs

            @pl.loop(first, first + pairs)
            def _(p):
                for t in range(n // 2):
                    a = lat_ref[2 * p, :, t * 128 : (t + 1) * 128]
                    b = lat_ref[2 * p + 1, :, t * 128 : (t + 1) * 128]
                    pack[2 * t, p] = jnp.concatenate([a[:, :64], b[:, :64]], axis=1)
                    pack[2 * t + 1, p] = jnp.concatenate([a[:, 64:], b[:, 64:]], axis=1)

        @pl.loop(1, n)
        def _(distance):
            peer = lax.rem(me + distance, n)
            piece(section, peer, me, peer).start()

        recv[pl.ds(section * pairs, pairs), me] = source(section, me)[...]

    for section in range(sections):

        @pl.loop(1, n)
        def _(distance):
            peer = lax.rem(me + n - distance, n)
            piece(section, peer, peer, peer).wait_recv()

        @pl.loop(section * quads, (section + 1) * quads)
        def _(q):
            pa = recv[2 * q].reshape(deep, 128)
            pb = recv[2 * q + 1].reshape(deep, 128)
            go_right[q] = jnp.concatenate([pa[:, 32:64], pa[:, 96:], pb[:, 32:64], pb[:, 96:]], axis=1)
            go_left[q] = jnp.concatenate([pa[:, :32], pa[:, 64:96], pb[:, :32], pb[:, 64:96]], axis=1)

        halo(section, 0).start()
        halo(section, 1).start()

    for section in range(sections):
        halo(section, 0).wait_recv()
        halo(section, 1).wait_recv()
    for section in range(sections):
        halo(section, 0).wait_send()
        halo(section, 1).wait_send()

        @pl.loop(1, n)
        def _(distance):
            peer = lax.rem(me + distance, n)
            piece(section, peer, me, peer).wait_send()


def exchanged(latent, axis):
    n = lax.axis_size(axis)
    rows, channels, _ = latent.shape
    pairs = rows // 2 + rows // 8
    quads = pairs // 2
    sections = 5
    deep = n * channels
    kind = latent.dtype
    vmem = pl.BlockSpec(memory_space=pltpu.VMEM)
    recv, from_left, from_right = pl.pallas_call(
        functools.partial(exchange, axis),
        out_shape=[
            jax.ShapeDtypeStruct((pairs, n, channels, 128), kind),
            jax.ShapeDtypeStruct((quads, deep, 128), kind),
            jax.ShapeDtypeStruct((quads, deep, 128), kind),
        ],
        in_specs=[vmem],
        out_specs=[vmem] * 3,
        scratch_shapes=[
            pltpu.VMEM((n, rows // 2, channels, 128), kind),
            pltpu.VMEM((quads, deep, 128), kind),
            pltpu.VMEM((quads, deep, 128), kind),
            pltpu.SemaphoreType.DMA((sections, n)),
            pltpu.SemaphoreType.DMA((sections, n)),
            pltpu.SemaphoreType.DMA((sections, 2)),
            pltpu.SemaphoreType.DMA((sections, 2)),
        ],
        compiler_params=pltpu.CompilerParams(
            collective_id=0, has_side_effects=True, vmem_limit_bytes=32 * 2**20
        ),
    )(latent)
    return recv.reshape(pairs, deep, 128), from_left, from_right


def spread(step, bases, entries, rows_ref, starts_ref, values_ref, out_ref, mixed):
    channels = out_ref.shape[2]
    for g in range(OUT_ROWS):
        h = step * OUT_ROWS + g
        parts = []
        for j in range(entries):
            e = h * entries + j
            start = pl.multiple_of(starts_ref[e], BLOCK)
            parts.append(mixed[rows_ref[e], pl.ds(start, 2 * BLOCK), :])
        first = jnp.concatenate([p[:BLOCK] for p in parts], axis=0)
        second = jnp.concatenate([p[BLOCK:] for p in parts], axis=0)
        terms = jnp.concatenate([first, second], axis=1)
        total = lax.dot_general(
            values_ref[g], terms, (((0,), (0,)), ((), ())), preferred_element_type=jnp.float32
        ).astype(jnp.bfloat16)
        out_ref[g, :FINE] = total[:, :channels]
        out_ref[g, FINE:] = total[:, channels:]


def compute_packed(mix_steps, bases, entries, rows_ref, starts_ref, quad_ref, own_ref, left_ref, right_ref, filt_ref, values_ref, out_ref, mixed):
    step = pl.program_id(0)
    channels = out_ref.shape[2]

    def mix(data, first_row, count, to):
        size = 128 // count
        product = lax.dot_general(
            data, filt_ref[...], (((0,), (0,)), ((), ())), preferred_element_type=jnp.float32
        )
        for r in range(count):
            row = first_row + r
            part = (product[r * size : (r + 1) * size] * quad_ref[row]).astype(jnp.bfloat16)
            for k in range(bases):
                mixed[row * bases + k, to : to + size] = part[:, k * channels : (k + 1) * channels]

    @pl.when(step < mix_steps)
    def _():
        mix(left_ref[0], step * 4, 4, 0)
        mix(own_ref[0], step * 4, 2, BLOCK)
        mix(own_ref[1], step * 4 + 2, 2, BLOCK)
        mix(right_ref[0], step * 4, 4, 3 * BLOCK)

    @pl.when(step >= mix_steps)
    def _():
        spread(step - mix_steps, bases, entries, rows_ref, starts_ref, values_ref, out_ref, mixed)


def on_device_packed(
    latent, filters, quadrature, basis_values, source_row, offset, basis_index, across_pole
):
    source_total = latent.shape[0]
    row_total, entries = source_row.shape
    bases, channels, deep = filters.shape
    pole = source_total // 4
    own, from_left, from_right = exchanged(latent, "lon")
    place = jnp.where((source_row >= pole) | (across_pole == 1), source_row + pole, source_row)
    rows = (place * bases + basis_index).reshape(-1)
    starts = ((1 - offset) * BLOCK).reshape(-1)
    quad = jnp.concatenate([quadrature[:pole], quadrature])
    filt = filters.reshape(bases * channels, deep).T
    values = jnp.swapaxes(basis_values, 2, 3).reshape(row_total, entries * BLOCK, FINE)
    all_rows = source_total + pole
    mix_steps = all_rows // 4
    out_steps = row_total // OUT_ROWS
    smem = pl.BlockSpec(memory_space=pltpu.SMEM)
    last = lambda i: jnp.maximum(i - mix_steps, 0)
    mixing = lambda i: (jnp.minimum(i, mix_steps - 1), 0, 0)
    return pl.pallas_call(
        functools.partial(compute_packed, mix_steps, bases, entries),
        grid=(mix_steps + out_steps,),
        out_shape=jax.ShapeDtypeStruct((row_total, 2 * FINE, channels), jnp.bfloat16),
        in_specs=[
            smem,
            smem,
            smem,
            pl.BlockSpec((2, deep, 128), mixing),
            pl.BlockSpec((1, deep, 128), mixing),
            pl.BlockSpec((1, deep, 128), mixing),
            pl.BlockSpec((deep, bases * channels), lambda i: (0, 0)),
            pl.BlockSpec((OUT_ROWS, entries * BLOCK, FINE), lambda i: (last(i), 0, 0)),
        ],
        out_specs=pl.BlockSpec((OUT_ROWS, 2 * FINE, channels), lambda i: (last(i), 0, 0)),
        scratch_shapes=[pltpu.VMEM((all_rows * bases, 4 * BLOCK, channels), jnp.bfloat16)],
        compiler_params=pltpu.CompilerParams(vmem_limit_bytes=48 * 2**20),
    )(rows, starts, quad, own, from_left, from_right, filt, values)


def solution(mesh):
    def chosen(latent, *rest):
        packed = latent.shape[1] % 16 == 0
        return (on_device_packed if packed else on_device)(latent, *rest)

    in_specs = (P("grp", "lon", None), P(), P(), P(), P(), P(), P(), P())
    out_specs = P("grp", "lon", None)
    return jax.shard_map(
        chosen, mesh=mesh, in_specs=in_specs, out_specs=out_specs, check_vma=False
    )
```

```python
import functools

import jax
import jax.numpy as jnp
from jax import lax
from jax.experimental import pallas as pl
from jax.experimental.pallas import tpu as pltpu
from jax.sharding import PartitionSpec as P

BLOCK = 32
FINE = 64
MIX_ROWS = 4
OUT_ROWS = 8
UNROLL = 4
MESH = pl.DeviceIdType.MESH


def from_behind(block, axis, distance):
    devices = range(lax.axis_size(axis))
    route = [((i - distance) % len(devices), i) for i in devices]
    return lax.ppermute(block, axis, route)


def compute(mix_steps, bases, entries, rows_ref, starts_ref, quad_ref, ext_ref, filt_ref, values_ref, out_ref, mixed):
    step = pl.program_id(0)
    channels = out_ref.shape[2]

    @pl.when(step < mix_steps)
    def _():
        for r in range(MIX_ROWS):
            row = step * MIX_ROWS + r
            product = lax.dot_general(
                ext_ref[r], filt_ref[...], (((0,), (0,)), ((), ())), preferred_element_type=jnp.float32
            )
            product = (product * quad_ref[row]).astype(jnp.bfloat16)
            for k in range(bases):
                mixed[row * bases + k] = product[:, k * channels : (k + 1) * channels]

    @pl.when(step >= mix_steps)
    def _():
        for g in range(OUT_ROWS):
            h = (step - mix_steps) * OUT_ROWS + g
            parts = []
            for j in range(entries):
                e = h * entries + j
                start = pl.multiple_of(starts_ref[e], BLOCK)
                parts.append(mixed[rows_ref[e], pl.ds(start, 2 * BLOCK), :])
            first = jnp.concatenate([p[:BLOCK] for p in parts], axis=0)
            second = jnp.concatenate([p[BLOCK:] for p in parts], axis=0)
            terms = jnp.concatenate([first, second], axis=1)
            values = jnp.concatenate([values_ref[g, j] for j in range(entries)], axis=1)
            total = jnp.dot(values, terms, preferred_element_type=jnp.float32)
            total = total.astype(jnp.bfloat16)
            out_ref[g, :FINE] = total[:, :channels]
            out_ref[g, FINE:] = total[:, channels:]


def on_device(
    latent, filters, quadrature, basis_values, source_row, offset, basis_index, across_pole
):
    source_total = latent.shape[0]
    row_total, entries = source_row.shape
    bases, channels, deep = filters.shape
    pole_source = source_total // 4
    half = latent.shape[2] // 2
    turned = jnp.roll(latent[:pole_source], half, axis=2)
    stacked = jnp.concatenate([latent, turned], axis=0)
    tile = lax.all_to_all(stacked, "lon", split_axis=2, concat_axis=1, tiled=True)
    left = from_behind(tile[:, :, BLOCK:], "lon", 1)
    right = from_behind(tile[:, :, :BLOCK], "lon", -1)
    ext = jnp.concatenate([left, tile, right], axis=2)
    rows = ((source_row + source_total * across_pole) * bases + basis_index).reshape(-1)
    starts = ((1 - offset) * BLOCK).reshape(-1)
    quad = jnp.concatenate([quadrature, quadrature[:pole_source]])
    filt = filters.reshape(bases * channels, deep).T
    all_rows = source_total + pole_source
    mix_steps = all_rows // MIX_ROWS
    out_steps = row_total // OUT_ROWS
    smem = pl.BlockSpec(memory_space=pltpu.SMEM)
    width = ext.shape[2]
    last = lambda i: jnp.maximum(i - mix_steps, 0)
    return pl.pallas_call(
        functools.partial(compute, mix_steps, bases, entries),
        grid=(mix_steps + out_steps,),
        out_shape=jax.ShapeDtypeStruct((row_total, 2 * FINE, channels), jnp.bfloat16),
        in_specs=[
            smem,
            smem,
            smem,
            pl.BlockSpec((MIX_ROWS, deep, width), lambda i: (jnp.minimum(i, mix_steps - 1), 0, 0)),
            pl.BlockSpec((deep, bases * channels), lambda i: (0, 0)),
            pl.BlockSpec((OUT_ROWS, entries, FINE, BLOCK), lambda i: (last(i), 0, 0, 0)),
        ],
        out_specs=pl.BlockSpec((OUT_ROWS, 2 * FINE, channels), lambda i: (last(i), 0, 0)),
        scratch_shapes=[pltpu.VMEM((all_rows * bases, width, channels), jnp.bfloat16)],
        compiler_params=pltpu.CompilerParams(vmem_limit_bytes=48 * 2**20),
    )(rows, starts, quad, ext, filt, basis_values)


def fused(axis, bases, entries, places_ref, quad_ref, lat_ref, filt_ref, values_ref, out_ref, recv, from_left, from_right, pack, go_right, go_left, turned, mixed, sends, recvs, halo_sends, halo_recvs):
    n = lax.axis_size(axis)
    me = lax.axis_index(axis)
    right, left = lax.rem(me + 1, n), lax.rem(me + n - 1, n)
    pairs = lat_ref.shape[0] // 8
    sections = lat_ref.shape[0] // (2 * pairs) + 1
    quads = pairs // 2
    deep = go_right.shape[1]
    channels = out_ref.shape[2]
    row_total = out_ref.shape[0]

    barrier = pltpu.get_barrier_semaphore()

    @pl.loop(1, n)
    def _(distance):
        peer = lax.rem(me + distance, n)
        pl.semaphore_signal(barrier, inc=1, device_id={axis: peer}, device_id_type=MESH)

    pl.semaphore_wait(barrier, n - 1)

    def source(section, target):
        if section == 1:
            return pack.at[lax.rem(target + n // 2, n), pl.ds(0, pairs)]
        return pack.at[target, pl.ds(max(section - 1, 0) * pairs, pairs)]

    def piece(section, target, sender, peer):
        return pltpu.make_async_remote_copy(
            src_ref=source(section, target),
            dst_ref=recv.at[pl.ds(section * pairs, pairs), sender],
            send_sem=sends.at[section, target],
            recv_sem=recvs.at[section, sender],
            device_id={axis: peer},
            device_id_type=MESH,
        )

    def halo(section, way):
        held, landed, peer = (go_right, from_left, right) if way == 0 else (go_left, from_right, left)
        part = pl.ds(section * quads, quads)
        return pltpu.make_async_remote_copy(
            src_ref=held.at[part],
            dst_ref=landed.at[part],
            send_sem=halo_sends.at[section, way],
            recv_sem=halo_recvs.at[section, way],
            device_id={axis: peer},
            device_id_type=MESH,
        )

    for section in range(sections):
        if section != 1:
            first = max(section - 1, 0) * pairs

            @pl.loop(first, first + pairs)
            def _(p):
                for t in range(n // 2):
                    a = lat_ref[2 * p, :, t * 128 : (t + 1) * 128]
                    b = lat_ref[2 * p + 1, :, t * 128 : (t + 1) * 128]
                    pack[2 * t, p] = jnp.concatenate([a[:, :64], b[:, :64]], axis=1)
                    pack[2 * t + 1, p] = jnp.concatenate([a[:, 64:], b[:, 64:]], axis=1)

        @pl.loop(1, n)
        def _(distance):
            peer = lax.rem(me + distance, n)
            piece(section, peer, me, peer).start()

        recv[pl.ds(section * pairs, pairs), me] = source(section, me)[...]

    @pl.loop(0, FINE)
    def _(u):
        flat = values_ref[:, u].reshape(entries * BLOCK, row_total).astype(jnp.float32).T
        for part in range(entries * BLOCK // 128):
            turned[part, pl.ds(u, row_total, stride=FINE), :] = flat[:, part * 128 : (part + 1) * 128]

    def mix(data, first_row, count, to):
        size = 128 // count
        product = lax.dot_general(
            data, filt_ref[...], (((0,), (0,)), ((), ())), preferred_element_type=jnp.float32
        )
        for r in range(count):
            row = first_row + r
            part = (product[r * size : (r + 1) * size] * quad_ref[row]).astype(jnp.bfloat16)
            for k in range(bases):
                for b in range(size // BLOCK):
                    mixed[(row * bases + k) * 4 + to + b] = part[
                        b * BLOCK : (b + 1) * BLOCK, k * channels : (k + 1) * channels
                    ]

    def finish(section):
        halo(section, 0).wait_recv()
        halo(section, 1).wait_recv()

        @pl.loop(section * quads, (section + 1) * quads)
        def _(q):
            mix(from_left[q], q * 4, 4, 0)
            mix(from_right[q], q * 4, 4, 3)

    def spread(begin, end):
        @pl.loop(begin // UNROLL, end // UNROLL)
        def _(group):
            for g in range(UNROLL):
                h = group * UNROLL + g
                at = [places_ref[h * entries + j] for j in range(entries)]
                first = jnp.concatenate([mixed[i] for i in at], axis=0)
                second = jnp.concatenate([mixed[i + 1] for i in at], axis=0)
                terms = jnp.concatenate([first, second], axis=1)
                here = pl.ds(pl.multiple_of(h * FINE, FINE), FINE)
                weights = jnp.concatenate([turned[i, here, :] for i in range(turned.shape[0])], axis=1)
                total = jnp.dot(weights.astype(jnp.bfloat16), terms, preferred_element_type=jnp.float32)
                total = total.astype(jnp.bfloat16)
                out_ref[h, :FINE] = total[:, :channels]
                out_ref[h, FINE:] = total[:, channels:]

    done = 0
    for section in range(sections):

        @pl.loop(1, n)
        def _(distance):
            peer = lax.rem(me + n - distance, n)
            piece(section, peer, peer, peer).wait_recv()

        @pl.loop(section * quads, (section + 1) * quads)
        def _(q):
            pa = recv[2 * q].reshape(deep, 128)
            pb = recv[2 * q + 1].reshape(deep, 128)
            go_right[q] = jnp.concatenate([pa[:, 32:64], pa[:, 96:], pb[:, 32:64], pb[:, 96:]], axis=1)
            go_left[q] = jnp.concatenate([pa[:, :32], pa[:, 64:96], pb[:, :32], pb[:, 64:96]], axis=1)

        halo(section, 0).start()
        halo(section, 1).start()

        @pl.loop(section * pairs, (section + 1) * pairs)
        def _(p):
            mix(recv[p].reshape(deep, 128), p * 2, 2, 1)

        if section >= 1:
            finish(section - 1)
        if section >= 3:
            ready = 4 * pairs * (section - 1) - 8
            spread(done, ready)
            done = ready

    finish(sections - 1)
    spread(done, row_total)
    for section in range(sections):
        halo(section, 0).wait_send()
        halo(section, 1).wait_send()

        @pl.loop(1, n)
        def _(distance):
            peer = lax.rem(me + distance, n)
            piece(section, peer, me, peer).wait_send()


def on_device_packed(
    latent, filters, quadrature, basis_values, source_row, offset, basis_index, across_pole
):
    n = lax.axis_size("lon")
    source_total = latent.shape[0]
    row_total, entries = source_row.shape
    bases, channels, deep = filters.shape
    pole = source_total // 4
    place = jnp.where((source_row >= pole) | (across_pole == 1), source_row + pole, source_row)
    places = ((place * bases + basis_index) * 4 + 1 - offset).reshape(-1)
    quad = jnp.concatenate([quadrature[:pole], quadrature])
    filt = filters.reshape(bases * channels, deep).T
    values = jnp.transpose(basis_values, (1, 2, 3, 0))
    all_rows = source_total + pole
    pairs, quads, sections = all_rows // 2, all_rows // 4, 5
    kind = latent.dtype
    smem = pl.BlockSpec(memory_space=pltpu.SMEM)
    vmem = pl.BlockSpec(memory_space=pltpu.VMEM)
    return pl.pallas_call(
        functools.partial(fused, "lon", bases, entries),
        out_shape=jax.ShapeDtypeStruct((row_total, 2 * FINE, channels), kind),
        in_specs=[smem, smem, vmem, vmem, vmem],
        out_specs=vmem,
        scratch_shapes=[
            pltpu.VMEM((pairs, n, latent.shape[1], 128), kind),
            pltpu.VMEM((quads, deep, 128), kind),
            pltpu.VMEM((quads, deep, 128), kind),
            pltpu.VMEM((n, source_total // 2, latent.shape[1], 128), kind),
            pltpu.VMEM((quads, deep, 128), kind),
            pltpu.VMEM((quads, deep, 128), kind),
            pltpu.VMEM((entries * BLOCK // 128, row_total * FINE, 128), jnp.float32),
            pltpu.VMEM((all_rows * bases * 4, BLOCK, channels), kind),
            pltpu.SemaphoreType.DMA((sections, n)),
            pltpu.SemaphoreType.DMA((sections, n)),
            pltpu.SemaphoreType.DMA((sections, 2)),
            pltpu.SemaphoreType.DMA((sections, 2)),
        ],
        compiler_params=pltpu.CompilerParams(
            collective_id=0, has_side_effects=True, vmem_limit_bytes=58 * 2**20
        ),
    )(places, quad, latent, filt, values)


def solution(mesh):
    def chosen(latent, *rest):
        packed = latent.shape[1] % 16 == 0
        return (on_device_packed if packed else on_device)(latent, *rest)

    in_specs = (P("grp", "lon", None), P(), P(), P(), P(), P(), P(), P())
    out_specs = P("grp", "lon", None)
    return jax.shard_map(
        chosen, mesh=mesh, in_specs=in_specs, out_specs=out_specs, check_vma=False
    )
```

```python
import functools

import jax
import jax.numpy as jnp
from jax import lax
from jax.experimental import pallas as pl
from jax.experimental.pallas import tpu as pltpu
from jax.sharding import PartitionSpec as P

BLOCK = 32
FINE = 64
MIX_ROWS = 4
OUT_ROWS = 8
UNROLL = 4
AHEAD = 3
MESH = pl.DeviceIdType.MESH


def from_behind(block, axis, distance):
    devices = range(lax.axis_size(axis))
    route = [((i - distance) % len(devices), i) for i in devices]
    return lax.ppermute(block, axis, route)


def compute(mix_steps, bases, entries, rows_ref, starts_ref, quad_ref, ext_ref, filt_ref, values_ref, out_ref, mixed):
    step = pl.program_id(0)
    channels = out_ref.shape[2]

    @pl.when(step < mix_steps)
    def _():
        for r in range(MIX_ROWS):
            row = step * MIX_ROWS + r
            product = lax.dot_general(
                ext_ref[r], filt_ref[...], (((0,), (0,)), ((), ())), preferred_element_type=jnp.float32
            )
            product = (product * quad_ref[row]).astype(jnp.bfloat16)
            for k in range(bases):
                mixed[row * bases + k] = product[:, k * channels : (k + 1) * channels]

    @pl.when(step >= mix_steps)
    def _():
        for g in range(OUT_ROWS):
            h = (step - mix_steps) * OUT_ROWS + g
            parts = []
            for j in range(entries):
                e = h * entries + j
                start = pl.multiple_of(starts_ref[e], BLOCK)
                parts.append(mixed[rows_ref[e], pl.ds(start, 2 * BLOCK), :])
            first = jnp.concatenate([p[:BLOCK] for p in parts], axis=0)
            second = jnp.concatenate([p[BLOCK:] for p in parts], axis=0)
            terms = jnp.concatenate([first, second], axis=1)
            values = jnp.concatenate([values_ref[g, j] for j in range(entries)], axis=1)
            total = jnp.dot(values, terms, preferred_element_type=jnp.float32)
            total = total.astype(jnp.bfloat16)
            out_ref[g, :FINE] = total[:, :channels]
            out_ref[g, FINE:] = total[:, channels:]


def on_device(
    latent, filters, quadrature, basis_values, source_row, offset, basis_index, across_pole
):
    source_total = latent.shape[0]
    row_total, entries = source_row.shape
    bases, channels, deep = filters.shape
    pole_source = source_total // 4
    half = latent.shape[2] // 2
    turned = jnp.roll(latent[:pole_source], half, axis=2)
    stacked = jnp.concatenate([latent, turned], axis=0)
    tile = lax.all_to_all(stacked, "lon", split_axis=2, concat_axis=1, tiled=True)
    left = from_behind(tile[:, :, BLOCK:], "lon", 1)
    right = from_behind(tile[:, :, :BLOCK], "lon", -1)
    ext = jnp.concatenate([left, tile, right], axis=2)
    rows = ((source_row + source_total * across_pole) * bases + basis_index).reshape(-1)
    starts = ((1 - offset) * BLOCK).reshape(-1)
    quad = jnp.concatenate([quadrature, quadrature[:pole_source]])
    filt = filters.reshape(bases * channels, deep).T
    all_rows = source_total + pole_source
    mix_steps = all_rows // MIX_ROWS
    out_steps = row_total // OUT_ROWS
    smem = pl.BlockSpec(memory_space=pltpu.SMEM)
    width = ext.shape[2]
    last = lambda i: jnp.maximum(i - mix_steps, 0)
    return pl.pallas_call(
        functools.partial(compute, mix_steps, bases, entries),
        grid=(mix_steps + out_steps,),
        out_shape=jax.ShapeDtypeStruct((row_total, 2 * FINE, channels), jnp.bfloat16),
        in_specs=[
            smem,
            smem,
            smem,
            pl.BlockSpec((MIX_ROWS, deep, width), lambda i: (jnp.minimum(i, mix_steps - 1), 0, 0)),
            pl.BlockSpec((deep, bases * channels), lambda i: (0, 0)),
            pl.BlockSpec((OUT_ROWS, entries, FINE, BLOCK), lambda i: (last(i), 0, 0, 0)),
        ],
        out_specs=pl.BlockSpec((OUT_ROWS, 2 * FINE, channels), lambda i: (last(i), 0, 0)),
        scratch_shapes=[pltpu.VMEM((all_rows * bases, width, channels), jnp.bfloat16)],
        compiler_params=pltpu.CompilerParams(vmem_limit_bytes=48 * 2**20),
    )(rows, starts, quad, ext, filt, basis_values)


def fused(axis, bases, entries, places_ref, quad_ref, lat_ref, filt_ref, values_hbm, out_ref, values_ref, filt_t, fetch_sem, recv, from_left, from_right, pack, go_right, go_left, turned, mixed, sends, recvs, halo_sends, halo_recvs):
    n = lax.axis_size(axis)
    me = lax.axis_index(axis)
    right, left = lax.rem(me + 1, n), lax.rem(me + n - 1, n)
    pairs = lat_ref.shape[0] // 8
    sections = lat_ref.shape[0] // (2 * pairs) + 1
    quads = pairs // 2
    deep = go_right.shape[1]
    channels = out_ref.shape[2]
    row_total = out_ref.shape[0]

    fetch = pltpu.make_async_copy(values_hbm, values_ref, fetch_sem)
    fetch.start()
    barrier = pltpu.get_barrier_semaphore()

    @pl.loop(1, n)
    def _(distance):
        peer = lax.rem(me + distance, n)
        pl.semaphore_signal(barrier, inc=1, device_id={axis: peer}, device_id_type=MESH)

    pl.semaphore_wait(barrier, n - 1)

    def source(section, target):
        if section == 1:
            return pack.at[lax.rem(target + n // 2, n), pl.ds(0, pairs)]
        return pack.at[target, pl.ds(max(section - 1, 0) * pairs, pairs)]

    def piece(section, target, sender, peer):
        return pltpu.make_async_remote_copy(
            src_ref=source(section, target),
            dst_ref=recv.at[pl.ds(section * pairs, pairs), sender],
            send_sem=sends.at[section, target],
            recv_sem=recvs.at[section, sender],
            device_id={axis: peer},
            device_id_type=MESH,
        )

    def halo(section, way):
        held, landed, peer = (go_right, from_left, right) if way == 0 else (go_left, from_right, left)
        part = pl.ds(section * quads, quads)
        return pltpu.make_async_remote_copy(
            src_ref=held.at[part],
            dst_ref=landed.at[part],
            send_sem=halo_sends.at[section, way],
            recv_sem=halo_recvs.at[section, way],
            device_id={axis: peer},
            device_id_type=MESH,
        )

    def send(section):
        @pl.loop(1, n)
        def _(distance):
            peer = lax.rem(me + distance * (n // 2 - 1), n)
            piece(section, peer, me, peer).start()

        recv[pl.ds(section * pairs, pairs), me] = source(section, me)[...]

    for section in range(sections):
        if section != 1:
            first = max(section - 1, 0) * pairs

            @pl.loop(first, first + pairs)
            def _(p):
                for t in range(n // 2):
                    a = lat_ref[2 * p, :, t * 128 : (t + 1) * 128]
                    b = lat_ref[2 * p + 1, :, t * 128 : (t + 1) * 128]
                    pack[2 * t, p] = jnp.concatenate([a[:, :64], b[:, :64]], axis=1)
                    pack[2 * t + 1, p] = jnp.concatenate([a[:, 64:], b[:, 64:]], axis=1)

        if section < AHEAD:
            send(section)

    fetch.wait()
    for k in range(bases):
        filt_t[:, k * channels : (k + 1) * channels] = filt_ref[k].astype(jnp.float32).T.astype(jnp.bfloat16)

    @pl.loop(0, FINE)
    def _(u):
        flat = values_ref[:, u].reshape(entries * BLOCK, row_total).astype(jnp.float32).T
        for part in range(entries * BLOCK // 128):
            turned[part, pl.ds(u, row_total, stride=FINE), :] = flat[:, part * 128 : (part + 1) * 128]

    def mix(data, first_row, count, to):
        size = 128 // count
        product = lax.dot_general(
            data, filt_t[...], (((0,), (0,)), ((), ())), preferred_element_type=jnp.float32
        )
        for r in range(count):
            row = first_row + r
            at = row - jnp.where(row >= 2 * pairs, 2 * pairs, 0)
            part = (product[r * size : (r + 1) * size] * quad_ref[at]).astype(jnp.bfloat16)
            for k in range(bases):
                for b in range(size // BLOCK):
                    mixed[(row * bases + k) * 4 + to + b] = part[
                        b * BLOCK : (b + 1) * BLOCK, k * channels : (k + 1) * channels
                    ]

    def finish(section):
        halo(section, 0).wait_recv()
        halo(section, 1).wait_recv()

        @pl.loop(section * quads, (section + 1) * quads)
        def _(q):
            mix(from_left[q], q * 4, 4, 0)
            mix(from_right[q], q * 4, 4, 3)

    def spread(begin, end):
        @pl.loop(begin // UNROLL, end // UNROLL)
        def _(group):
            for g in range(UNROLL):
                h = group * UNROLL + g
                at = [places_ref[h * entries + j] for j in range(entries)]
                first = jnp.concatenate([mixed[i] for i in at], axis=0)
                second = jnp.concatenate([mixed[i + 1] for i in at], axis=0)
                terms = jnp.concatenate([first, second], axis=1)
                here = pl.ds(pl.multiple_of(h * FINE, FINE), FINE)
                weights = jnp.concatenate([turned[i, here, :] for i in range(turned.shape[0])], axis=1)
                total = jnp.dot(weights.astype(jnp.bfloat16), terms, preferred_element_type=jnp.float32)
                total = total.astype(jnp.bfloat16)
                out_ref[h, :FINE] = total[:, :channels]
                out_ref[h, FINE:] = total[:, channels:]

    done = 0
    for section in range(sections):

        @pl.loop(1, n)
        def _(distance):
            peer = lax.rem(me + n - distance, n)
            piece(section, peer, peer, peer).wait_recv()

        @pl.loop(section * quads, (section + 1) * quads)
        def _(q):
            pa = recv[2 * q].reshape(deep, 128)
            pb = recv[2 * q + 1].reshape(deep, 128)
            go_right[q] = jnp.concatenate([pa[:, 32:64], pa[:, 96:], pb[:, 32:64], pb[:, 96:]], axis=1)
            go_left[q] = jnp.concatenate([pa[:, :32], pa[:, 64:96], pb[:, :32], pb[:, 64:96]], axis=1)

        halo(section, 0).start()
        halo(section, 1).start()
        if section + AHEAD < sections:
            send(section + AHEAD)

        @pl.loop(section * pairs, (section + 1) * pairs)
        def _(p):
            mix(recv[p].reshape(deep, 128), p * 2, 2, 1)

        if section >= 1:
            finish(section - 1)
        if section >= 3:
            ready = 4 * pairs * (section - 1) - 8
            spread(done, ready)
            done = ready

    finish(sections - 1)
    spread(done, row_total)
    for section in range(sections):
        halo(section, 0).wait_send()
        halo(section, 1).wait_send()

        @pl.loop(1, n)
        def _(distance):
            peer = lax.rem(me + distance, n)
            piece(section, peer, me, peer).wait_send()


def on_device_packed(
    latent, filters, quadrature, basis_values, source_row, offset, basis_index, across_pole
):
    n = lax.axis_size("lon")
    source_total = latent.shape[0]
    row_total, entries = source_row.shape
    bases, channels, deep = filters.shape
    pole = source_total // 4
    place = jnp.where((source_row >= pole) | (across_pole == 1), source_row + pole, source_row)
    places = ((place * bases + basis_index) * 4 + 1 - offset).reshape(-1)
    values = jnp.transpose(basis_values, (1, 2, 3, 0))
    all_rows = source_total + pole
    pairs, quads, sections = all_rows // 2, all_rows // 4, 5
    kind = latent.dtype
    smem = pl.BlockSpec(memory_space=pltpu.SMEM)
    vmem = pl.BlockSpec(memory_space=pltpu.VMEM)
    return pl.pallas_call(
        functools.partial(fused, "lon", bases, entries),
        out_shape=jax.ShapeDtypeStruct((row_total, 2 * FINE, channels), kind),
        in_specs=[smem, smem, vmem, vmem, pl.BlockSpec(memory_space=pl.ANY)],
        out_specs=vmem,
        scratch_shapes=[
            pltpu.VMEM(values.shape, kind),
            pltpu.VMEM((deep, bases * channels), kind),
            pltpu.SemaphoreType.DMA,
            pltpu.VMEM((pairs, n, latent.shape[1], 128), kind),
            pltpu.VMEM((quads, deep, 128), kind),
            pltpu.VMEM((quads, deep, 128), kind),
            pltpu.VMEM((n, source_total // 2, latent.shape[1], 128), kind),
            pltpu.VMEM((quads, deep, 128), kind),
            pltpu.VMEM((quads, deep, 128), kind),
            pltpu.VMEM((entries * BLOCK // 128, row_total * FINE, 128), jnp.float32),
            pltpu.VMEM((all_rows * bases * 4, BLOCK, channels), kind),
            pltpu.SemaphoreType.DMA((sections, n)),
            pltpu.SemaphoreType.DMA((sections, n)),
            pltpu.SemaphoreType.DMA((sections, 2)),
            pltpu.SemaphoreType.DMA((sections, 2)),
        ],
        compiler_params=pltpu.CompilerParams(
            collective_id=0, has_side_effects=True, vmem_limit_bytes=58 * 2**20
        ),
    )(places, quadrature, latent, filters, values)


def solution(mesh):
    def chosen(latent, *rest):
        packed = latent.shape[1] % 16 == 0
        return (on_device_packed if packed else on_device)(latent, *rest)

    in_specs = (P("grp", "lon", None), P(), P(), P(), P(), P(), P(), P())
    out_specs = P("grp", "lon", None)
    return jax.shard_map(
        chosen, mesh=mesh, in_specs=in_specs, out_specs=out_specs, check_vma=False
    )
```

```python
import functools

import jax
import jax.numpy as jnp
from jax import lax
from jax.experimental import pallas as pl
from jax.experimental.pallas import tpu as pltpu
from jax.sharding import PartitionSpec as P

BLOCK = 32
FINE = 64
MIX_ROWS = 4
OUT_ROWS = 8
UNROLL = 4
AHEAD = 3
MESH = pl.DeviceIdType.MESH


def from_behind(block, axis, distance):
    devices = range(lax.axis_size(axis))
    route = [((i - distance) % len(devices), i) for i in devices]
    return lax.ppermute(block, axis, route)


def compute(mix_steps, bases, entries, rows_ref, starts_ref, quad_ref, ext_ref, filt_ref, values_ref, out_ref, mixed):
    step = pl.program_id(0)
    channels = out_ref.shape[2]

    @pl.when(step < mix_steps)
    def _():
        for r in range(MIX_ROWS):
            row = step * MIX_ROWS + r
            product = lax.dot_general(
                ext_ref[r], filt_ref[...], (((0,), (0,)), ((), ())), preferred_element_type=jnp.float32
            )
            product = (product * quad_ref[row]).astype(jnp.bfloat16)
            for k in range(bases):
                mixed[row * bases + k] = product[:, k * channels : (k + 1) * channels]

    @pl.when(step >= mix_steps)
    def _():
        for g in range(OUT_ROWS):
            h = (step - mix_steps) * OUT_ROWS + g
            parts = []
            for j in range(entries):
                e = h * entries + j
                start = pl.multiple_of(starts_ref[e], BLOCK)
                parts.append(mixed[rows_ref[e], pl.ds(start, 2 * BLOCK), :])
            first = jnp.concatenate([p[:BLOCK] for p in parts], axis=0)
            second = jnp.concatenate([p[BLOCK:] for p in parts], axis=0)
            terms = jnp.concatenate([first, second], axis=1)
            values = jnp.concatenate([values_ref[g, j] for j in range(entries)], axis=1)
            total = jnp.dot(values, terms, preferred_element_type=jnp.float32)
            total = total.astype(jnp.bfloat16)
            out_ref[g, :FINE] = total[:, :channels]
            out_ref[g, FINE:] = total[:, channels:]


def on_device(
    latent, filters, quadrature, basis_values, source_row, offset, basis_index, across_pole
):
    source_total = latent.shape[0]
    row_total, entries = source_row.shape
    bases, channels, deep = filters.shape
    pole_source = source_total // 4
    half = latent.shape[2] // 2
    turned = jnp.roll(latent[:pole_source], half, axis=2)
    stacked = jnp.concatenate([latent, turned], axis=0)
    tile = lax.all_to_all(stacked, "lon", split_axis=2, concat_axis=1, tiled=True)
    left = from_behind(tile[:, :, BLOCK:], "lon", 1)
    right = from_behind(tile[:, :, :BLOCK], "lon", -1)
    ext = jnp.concatenate([left, tile, right], axis=2)
    rows = ((source_row + source_total * across_pole) * bases + basis_index).reshape(-1)
    starts = ((1 - offset) * BLOCK).reshape(-1)
    quad = jnp.concatenate([quadrature, quadrature[:pole_source]])
    filt = filters.reshape(bases * channels, deep).T
    all_rows = source_total + pole_source
    mix_steps = all_rows // MIX_ROWS
    out_steps = row_total // OUT_ROWS
    smem = pl.BlockSpec(memory_space=pltpu.SMEM)
    width = ext.shape[2]
    last = lambda i: jnp.maximum(i - mix_steps, 0)
    return pl.pallas_call(
        functools.partial(compute, mix_steps, bases, entries),
        grid=(mix_steps + out_steps,),
        out_shape=jax.ShapeDtypeStruct((row_total, 2 * FINE, channels), jnp.bfloat16),
        in_specs=[
            smem,
            smem,
            smem,
            pl.BlockSpec((MIX_ROWS, deep, width), lambda i: (jnp.minimum(i, mix_steps - 1), 0, 0)),
            pl.BlockSpec((deep, bases * channels), lambda i: (0, 0)),
            pl.BlockSpec((OUT_ROWS, entries, FINE, BLOCK), lambda i: (last(i), 0, 0, 0)),
        ],
        out_specs=pl.BlockSpec((OUT_ROWS, 2 * FINE, channels), lambda i: (last(i), 0, 0)),
        scratch_shapes=[pltpu.VMEM((all_rows * bases, width, channels), jnp.bfloat16)],
        compiler_params=pltpu.CompilerParams(vmem_limit_bytes=48 * 2**20),
    )(rows, starts, quad, ext, filt, basis_values)


def fused(axis, bases, entries, places_ref, quad_ref, lat_ref, filt_ref, values_hbm, out_ref, values_ref, filt_t, fetch_sem, recv, from_left, from_right, pack, go_right, go_left, turned, mixed, sends, recvs, halo_sends, halo_recvs):
    n = lax.axis_size(axis)
    me = lax.axis_index(axis)
    right, left = lax.rem(me + 1, n), lax.rem(me + n - 1, n)
    pairs = lat_ref.shape[0] // 8
    small = pairs // 2
    cuts = [(0, pairs, 0), (pairs, pairs, 0), (2 * pairs, pairs, pairs), (3 * pairs, pairs, 2 * pairs)]
    cuts += [(4 * pairs, small, 3 * pairs), (4 * pairs + small, small, 3 * pairs + small)]
    sections = len(cuts)
    deep = go_right.shape[1]
    channels = out_ref.shape[2]
    row_total = out_ref.shape[0]

    fetch = pltpu.make_async_copy(values_hbm, values_ref, fetch_sem)
    fetch.start()
    barrier = pltpu.get_barrier_semaphore()

    @pl.loop(1, n)
    def _(distance):
        peer = lax.rem(me + distance, n)
        pl.semaphore_signal(barrier, inc=1, device_id={axis: peer}, device_id_type=MESH)

    pl.semaphore_wait(barrier, n - 1)

    def source(section, target):
        if section == 1:
            target = lax.rem(target + n // 2, n)
        return pack.at[target, pl.ds(cuts[section][2], cuts[section][1])]

    def piece(section, target, sender, peer):
        return pltpu.make_async_remote_copy(
            src_ref=source(section, target),
            dst_ref=recv.at[pl.ds(cuts[section][0], cuts[section][1]), sender],
            send_sem=sends.at[section, target],
            recv_sem=recvs.at[section, sender],
            device_id={axis: peer},
            device_id_type=MESH,
        )

    def halo(section, way):
        held, landed, peer = (go_right, from_left, right) if way == 0 else (go_left, from_right, left)
        part = pl.ds(cuts[section][0] // 2, cuts[section][1] // 2)
        return pltpu.make_async_remote_copy(
            src_ref=held.at[part],
            dst_ref=landed.at[part],
            send_sem=halo_sends.at[section, way],
            recv_sem=halo_recvs.at[section, way],
            device_id={axis: peer},
            device_id_type=MESH,
        )

    def send(section):
        @pl.loop(1, n)
        def _(distance):
            peer = lax.rem(me + distance * (n // 2 - 1), n)
            piece(section, peer, me, peer).start()

        recv[pl.ds(cuts[section][0], cuts[section][1]), me] = source(section, me)[...]

    for section in range(sections):
        if section != 1:

            @pl.loop(cuts[section][2], cuts[section][2] + cuts[section][1])
            def _(p):
                for t in range(n // 2):
                    a = lat_ref[2 * p, :, t * 128 : (t + 1) * 128]
                    b = lat_ref[2 * p + 1, :, t * 128 : (t + 1) * 128]
                    pack[2 * t, p] = jnp.concatenate([a[:, :64], b[:, :64]], axis=1)
                    pack[2 * t + 1, p] = jnp.concatenate([a[:, 64:], b[:, 64:]], axis=1)

        if section < AHEAD:
            send(section)

    fetch.wait()
    for k in range(bases):
        filt_t[:, k * channels : (k + 1) * channels] = filt_ref[k].astype(jnp.float32).T.astype(jnp.bfloat16)

    @pl.loop(0, FINE)
    def _(u):
        flat = values_ref[:, u].reshape(entries * BLOCK, row_total).astype(jnp.float32).T
        for part in range(entries * BLOCK // 128):
            turned[part, pl.ds(u, row_total, stride=FINE), :] = flat[:, part * 128 : (part + 1) * 128]

    def mix(data, first_row, count, to):
        size = 128 // count
        product = lax.dot_general(
            data, filt_t[...], (((0,), (0,)), ((), ())), preferred_element_type=jnp.float32
        )
        for r in range(count):
            row = first_row + r
            at = row - jnp.where(row >= 2 * pairs, 2 * pairs, 0)
            part = (product[r * size : (r + 1) * size] * quad_ref[at]).astype(jnp.bfloat16)
            for k in range(bases):
                for b in range(size // BLOCK):
                    mixed[(row * bases + k) * 4 + to + b] = part[
                        b * BLOCK : (b + 1) * BLOCK, k * channels : (k + 1) * channels
                    ]

    def finish(section):
        halo(section, 0).wait_recv()
        halo(section, 1).wait_recv()

        @pl.loop(cuts[section][0] // 2, (cuts[section][0] + cuts[section][1]) // 2)
        def _(q):
            mix(from_left[q], q * 4, 4, 0)
            mix(from_right[q], q * 4, 4, 3)

    def spread(begin, end):
        @pl.loop(begin // UNROLL, end // UNROLL)
        def _(group):
            for g in range(UNROLL):
                h = group * UNROLL + g
                at = [places_ref[h * entries + j] for j in range(entries)]
                first = jnp.concatenate([mixed[i] for i in at], axis=0)
                second = jnp.concatenate([mixed[i + 1] for i in at], axis=0)
                terms = jnp.concatenate([first, second], axis=1)
                here = pl.ds(pl.multiple_of(h * FINE, FINE), FINE)
                weights = jnp.concatenate([turned[i, here, :] for i in range(turned.shape[0])], axis=1)
                total = jnp.dot(weights.astype(jnp.bfloat16), terms, preferred_element_type=jnp.float32)
                total = total.astype(jnp.bfloat16)
                out_ref[h, :FINE] = total[:, :channels]
                out_ref[h, FINE:] = total[:, channels:]

    done = 0
    for section in range(sections):

        @pl.loop(1, n)
        def _(distance):
            peer = lax.rem(me + n - distance, n)
            piece(section, peer, peer, peer).wait_recv()

        @pl.loop(cuts[section][0] // 2, (cuts[section][0] + cuts[section][1]) // 2)
        def _(q):
            pa = recv[2 * q].reshape(deep, 128)
            pb = recv[2 * q + 1].reshape(deep, 128)
            go_right[q] = jnp.concatenate([pa[:, 32:64], pa[:, 96:], pb[:, 32:64], pb[:, 96:]], axis=1)
            go_left[q] = jnp.concatenate([pa[:, :32], pa[:, 64:96], pb[:, :32], pb[:, 64:96]], axis=1)

        halo(section, 0).start()
        halo(section, 1).start()
        if section + AHEAD < sections:
            send(section + AHEAD)

        @pl.loop(cuts[section][0], cuts[section][0] + cuts[section][1])
        def _(p):
            mix(recv[p].reshape(deep, 128), p * 2, 2, 1)

        if section >= 1:
            finish(section - 1)
        if section >= 3:
            ready = 4 * cuts[section][2] - 8
            spread(done, ready)
            done = ready

    finish(sections - 1)
    spread(done, row_total)
    for section in range(sections):
        halo(section, 0).wait_send()
        halo(section, 1).wait_send()

        @pl.loop(1, n)
        def _(distance):
            peer = lax.rem(me + distance, n)
            piece(section, peer, me, peer).wait_send()


def on_device_packed(
    latent, filters, quadrature, basis_values, source_row, offset, basis_index, across_pole
):
    n = lax.axis_size("lon")
    source_total = latent.shape[0]
    row_total, entries = source_row.shape
    bases, channels, deep = filters.shape
    pole = source_total // 4
    place = jnp.where((source_row >= pole) | (across_pole == 1), source_row + pole, source_row)
    places = ((place * bases + basis_index) * 4 + 1 - offset).reshape(-1)
    values = jnp.transpose(basis_values, (1, 2, 3, 0))
    all_rows = source_total + pole
    pairs, quads, sections = all_rows // 2, all_rows // 4, 6
    kind = latent.dtype
    smem = pl.BlockSpec(memory_space=pltpu.SMEM)
    vmem = pl.BlockSpec(memory_space=pltpu.VMEM)
    return pl.pallas_call(
        functools.partial(fused, "lon", bases, entries),
        out_shape=jax.ShapeDtypeStruct((row_total, 2 * FINE, channels), kind),
        in_specs=[smem, smem, vmem, vmem, pl.BlockSpec(memory_space=pl.ANY)],
        out_specs=vmem,
        scratch_shapes=[
            pltpu.VMEM(values.shape, kind),
            pltpu.VMEM((deep, bases * channels), kind),
            pltpu.SemaphoreType.DMA,
            pltpu.VMEM((pairs, n, latent.shape[1], 128), kind),
            pltpu.VMEM((quads, deep, 128), kind),
            pltpu.VMEM((quads, deep, 128), kind),
            pltpu.VMEM((n, source_total // 2, latent.shape[1], 128), kind),
            pltpu.VMEM((quads, deep, 128), kind),
            pltpu.VMEM((quads, deep, 128), kind),
            pltpu.VMEM((entries * BLOCK // 128, row_total * FINE, 128), jnp.float32),
            pltpu.VMEM((all_rows * bases * 4, BLOCK, channels), kind),
            pltpu.SemaphoreType.DMA((sections, n)),
            pltpu.SemaphoreType.DMA((sections, n)),
            pltpu.SemaphoreType.DMA((sections, 2)),
            pltpu.SemaphoreType.DMA((sections, 2)),
        ],
        compiler_params=pltpu.CompilerParams(
            collective_id=0, has_side_effects=True, vmem_limit_bytes=58 * 2**20
        ),
    )(places, quadrature, latent, filters, values)


def solution(mesh):
    def chosen(latent, *rest):
        packed = latent.shape[1] % 16 == 0
        return (on_device_packed if packed else on_device)(latent, *rest)

    in_specs = (P("grp", "lon", None), P(), P(), P(), P(), P(), P(), P())
    out_specs = P("grp", "lon", None)
    return jax.shard_map(
        chosen, mesh=mesh, in_specs=in_specs, out_specs=out_specs, check_vma=False
    )
```

```python
import functools

import jax
import jax.numpy as jnp
from jax import lax
from jax.experimental import pallas as pl
from jax.experimental.pallas import tpu as pltpu
from jax.sharding import PartitionSpec as P

BLOCK = 32
FINE = 64
MIX_ROWS = 4
OUT_ROWS = 8
UNROLL = 4
AHEAD = 2
MESH = pl.DeviceIdType.MESH


def from_behind(block, axis, distance):
    devices = range(lax.axis_size(axis))
    route = [((i - distance) % len(devices), i) for i in devices]
    return lax.ppermute(block, axis, route)


def compute(mix_steps, bases, entries, rows_ref, starts_ref, quad_ref, ext_ref, filt_ref, values_ref, out_ref, mixed):
    step = pl.program_id(0)
    channels = out_ref.shape[2]

    @pl.when(step < mix_steps)
    def _():
        for r in range(MIX_ROWS):
            row = step * MIX_ROWS + r
            product = lax.dot_general(
                ext_ref[r], filt_ref[...], (((0,), (0,)), ((), ())), preferred_element_type=jnp.float32
            )
            product = (product * quad_ref[row]).astype(jnp.bfloat16)
            for k in range(bases):
                mixed[row * bases + k] = product[:, k * channels : (k + 1) * channels]

    @pl.when(step >= mix_steps)
    def _():
        for g in range(OUT_ROWS):
            h = (step - mix_steps) * OUT_ROWS + g
            parts = []
            for j in range(entries):
                e = h * entries + j
                start = pl.multiple_of(starts_ref[e], BLOCK)
                parts.append(mixed[rows_ref[e], pl.ds(start, 2 * BLOCK), :])
            first = jnp.concatenate([p[:BLOCK] for p in parts], axis=0)
            second = jnp.concatenate([p[BLOCK:] for p in parts], axis=0)
            terms = jnp.concatenate([first, second], axis=1)
            values = jnp.concatenate([values_ref[g, j] for j in range(entries)], axis=1)
            total = jnp.dot(values, terms, preferred_element_type=jnp.float32)
            total = total.astype(jnp.bfloat16)
            out_ref[g, :FINE] = total[:, :channels]
            out_ref[g, FINE:] = total[:, channels:]


def on_device(
    latent, filters, quadrature, basis_values, source_row, offset, basis_index, across_pole
):
    source_total = latent.shape[0]
    row_total, entries = source_row.shape
    bases, channels, deep = filters.shape
    pole_source = source_total // 4
    half = latent.shape[2] // 2
    turned = jnp.roll(latent[:pole_source], half, axis=2)
    stacked = jnp.concatenate([latent, turned], axis=0)
    tile = lax.all_to_all(stacked, "lon", split_axis=2, concat_axis=1, tiled=True)
    left = from_behind(tile[:, :, BLOCK:], "lon", 1)
    right = from_behind(tile[:, :, :BLOCK], "lon", -1)
    ext = jnp.concatenate([left, tile, right], axis=2)
    rows = ((source_row + source_total * across_pole) * bases + basis_index).reshape(-1)
    starts = ((1 - offset) * BLOCK).reshape(-1)
    quad = jnp.concatenate([quadrature, quadrature[:pole_source]])
    filt = filters.reshape(bases * channels, deep).T
    all_rows = source_total + pole_source
    mix_steps = all_rows // MIX_ROWS
    out_steps = row_total // OUT_ROWS
    smem = pl.BlockSpec(memory_space=pltpu.SMEM)
    width = ext.shape[2]
    last = lambda i: jnp.maximum(i - mix_steps, 0)
    return pl.pallas_call(
        functools.partial(compute, mix_steps, bases, entries),
        grid=(mix_steps + out_steps,),
        out_shape=jax.ShapeDtypeStruct((row_total, 2 * FINE, channels), jnp.bfloat16),
        in_specs=[
            smem,
            smem,
            smem,
            pl.BlockSpec((MIX_ROWS, deep, width), lambda i: (jnp.minimum(i, mix_steps - 1), 0, 0)),
            pl.BlockSpec((deep, bases * channels), lambda i: (0, 0)),
            pl.BlockSpec((OUT_ROWS, entries, FINE, BLOCK), lambda i: (last(i), 0, 0, 0)),
        ],
        out_specs=pl.BlockSpec((OUT_ROWS, 2 * FINE, channels), lambda i: (last(i), 0, 0)),
        scratch_shapes=[pltpu.VMEM((all_rows * bases, width, channels), jnp.bfloat16)],
        compiler_params=pltpu.CompilerParams(vmem_limit_bytes=48 * 2**20),
    )(rows, starts, quad, ext, filt, basis_values)


def fused(axis, bases, entries, places_ref, quad_ref, lat_ref, filt_ref, values_hbm, out_ref, values_ref, filt_t, fetch_sem, recv, from_left, from_right, pack, go_right, go_left, turned, mixed, sends, recvs, halo_sends, halo_recvs):
    n = lax.axis_size(axis)
    me = lax.axis_index(axis)
    right, left = lax.rem(me + 1, n), lax.rem(me + n - 1, n)
    pairs = lat_ref.shape[0] // 8
    sections = lat_ref.shape[0] // (2 * pairs) + 1
    quads = pairs // 2
    deep = go_right.shape[1]
    channels = out_ref.shape[2]
    row_total = out_ref.shape[0]

    fetch = pltpu.make_async_copy(values_hbm, values_ref, fetch_sem)
    fetch.start()
    barrier = pltpu.get_barrier_semaphore()

    @pl.loop(1, n)
    def _(distance):
        peer = lax.rem(me + distance, n)
        pl.semaphore_signal(barrier, inc=1, device_id={axis: peer}, device_id_type=MESH)

    pl.semaphore_wait(barrier, n - 1)

    def source(section, target):
        if section == 1:
            return pack.at[lax.rem(target + n // 2, n), pl.ds(0, pairs)]
        return pack.at[target, pl.ds(max(section - 1, 0) * pairs, pairs)]

    def piece(section, target, sender, peer):
        return pltpu.make_async_remote_copy(
            src_ref=source(section, target),
            dst_ref=recv.at[pl.ds(section * pairs, pairs), sender],
            send_sem=sends.at[section, target],
            recv_sem=recvs.at[section, sender],
            device_id={axis: peer},
            device_id_type=MESH,
        )

    def halo(section, way):
        held, landed, peer = (go_right, from_left, right) if way == 0 else (go_left, from_right, left)
        part = pl.ds(section * quads, quads)
        return pltpu.make_async_remote_copy(
            src_ref=held.at[part],
            dst_ref=landed.at[part],
            send_sem=halo_sends.at[section, way],
            recv_sem=halo_recvs.at[section, way],
            device_id={axis: peer},
            device_id_type=MESH,
        )

    def send(section):
        @pl.loop(1, n)
        def _(distance):
            peer = lax.rem(me + distance * (n // 2 - 1), n)
            piece(section, peer, me, peer).start()

        recv[pl.ds(section * pairs, pairs), me] = source(section, me)[...]

    for section in range(sections):
        if section != 1:
            first = max(section - 1, 0) * pairs

            @pl.loop(first, first + pairs)
            def _(p):
                for t in range(n // 2):
                    a = lat_ref[2 * p, :, t * 128 : (t + 1) * 128]
                    b = lat_ref[2 * p + 1, :, t * 128 : (t + 1) * 128]
                    pack[2 * t, p] = jnp.concatenate([a[:, :64], b[:, :64]], axis=1)
                    pack[2 * t + 1, p] = jnp.concatenate([a[:, 64:], b[:, 64:]], axis=1)

        if section < AHEAD:
            send(section)

    fetch.wait()
    for k in range(bases):
        filt_t[:, k * channels : (k + 1) * channels] = filt_ref[k].astype(jnp.float32).T.astype(jnp.bfloat16)

    @pl.loop(0, FINE)
    def _(u):
        flat = values_ref[:, u].reshape(entries * BLOCK, row_total).astype(jnp.float32).T
        for part in range(entries * BLOCK // 128):
            turned[part, pl.ds(u, row_total, stride=FINE), :] = flat[:, part * 128 : (part + 1) * 128]

    def mix(data, first_row, count, to):
        size = 128 // count
        product = lax.dot_general(
            data, filt_t[...], (((0,), (0,)), ((), ())), preferred_element_type=jnp.float32
        )
        for r in range(count):
            row = first_row + r
            at = row - jnp.where(row >= 2 * pairs, 2 * pairs, 0)
            part = (product[r * size : (r + 1) * size] * quad_ref[at]).astype(jnp.bfloat16)
            for k in range(bases):
                for b in range(size // BLOCK):
                    mixed[(row * bases + k) * 4 + to + b] = part[
                        b * BLOCK : (b + 1) * BLOCK, k * channels : (k + 1) * channels
                    ]

    def finish(section):
        halo(section, 0).wait_recv()
        halo(section, 1).wait_recv()

        @pl.loop(section * quads, (section + 1) * quads)
        def _(q):
            mix(from_left[q], q * 4, 4, 0)
            mix(from_right[q], q * 4, 4, 3)

    def spread(begin, end):
        @pl.loop(begin // UNROLL, end // UNROLL)
        def _(group):
            for g in range(UNROLL):
                h = group * UNROLL + g
                at = [places_ref[h * entries + j] for j in range(entries)]
                first = jnp.concatenate([mixed[i] for i in at], axis=0)
                second = jnp.concatenate([mixed[i + 1] for i in at], axis=0)
                terms = jnp.concatenate([first, second], axis=1)
                here = pl.ds(pl.multiple_of(h * FINE, FINE), FINE)
                weights = jnp.concatenate([turned[i, here, :] for i in range(turned.shape[0])], axis=1)
                total = jnp.dot(weights.astype(jnp.bfloat16), terms, preferred_element_type=jnp.float32)
                total = total.astype(jnp.bfloat16)
                out_ref[h, :FINE] = total[:, :channels]
                out_ref[h, FINE:] = total[:, channels:]

    done = 0
    for section in range(sections):

        @pl.loop(1, n)
        def _(distance):
            peer = lax.rem(me + n - distance, n)
            piece(section, peer, peer, peer).wait_recv()

        @pl.loop(section * quads, (section + 1) * quads)
        def _(q):
            pa = recv[2 * q].reshape(deep, 128)
            pb = recv[2 * q + 1].reshape(deep, 128)
            go_right[q] = jnp.concatenate([pa[:, 32:64], pa[:, 96:], pb[:, 32:64], pb[:, 96:]], axis=1)
            go_left[q] = jnp.concatenate([pa[:, :32], pa[:, 64:96], pb[:, :32], pb[:, 64:96]], axis=1)

        halo(section, 0).start()
        halo(section, 1).start()
        if section + AHEAD < sections:
            send(section + AHEAD)

        @pl.loop(section * pairs, (section + 1) * pairs)
        def _(p):
            mix(recv[p].reshape(deep, 128), p * 2, 2, 1)

        if section >= 1:
            finish(section - 1)
        if section >= 3:
            ready = 4 * pairs * (section - 1) - 8
            spread(done, ready)
            done = ready

    finish(sections - 1)
    spread(done, row_total)
    for section in range(sections):
        halo(section, 0).wait_send()
        halo(section, 1).wait_send()

        @pl.loop(1, n)
        def _(distance):
            peer = lax.rem(me + distance, n)
            piece(section, peer, me, peer).wait_send()


def on_device_packed(
    latent, filters, quadrature, basis_values, source_row, offset, basis_index, across_pole
):
    n = lax.axis_size("lon")
    source_total = latent.shape[0]
    row_total, entries = source_row.shape
    bases, channels, deep = filters.shape
    pole = source_total // 4
    place = jnp.where((source_row >= pole) | (across_pole == 1), source_row + pole, source_row)
    places = ((place * bases + basis_index) * 4 + 1 - offset).reshape(-1)
    values = jnp.transpose(basis_values, (1, 2, 3, 0))
    all_rows = source_total + pole
    pairs, quads, sections = all_rows // 2, all_rows // 4, 5
    kind = latent.dtype
    smem = pl.BlockSpec(memory_space=pltpu.SMEM)
    vmem = pl.BlockSpec(memory_space=pltpu.VMEM)
    return pl.pallas_call(
        functools.partial(fused, "lon", bases, entries),
        out_shape=jax.ShapeDtypeStruct((row_total, 2 * FINE, channels), kind),
        in_specs=[smem, smem, vmem, vmem, pl.BlockSpec(memory_space=pl.ANY)],
        out_specs=vmem,
        scratch_shapes=[
            pltpu.VMEM(values.shape, kind),
            pltpu.VMEM((deep, bases * channels), kind),
            pltpu.SemaphoreType.DMA,
            pltpu.VMEM((pairs, n, latent.shape[1], 128), kind),
            pltpu.VMEM((quads, deep, 128), kind),
            pltpu.VMEM((quads, deep, 128), kind),
            pltpu.VMEM((n, source_total // 2, latent.shape[1], 128), kind),
            pltpu.VMEM((quads, deep, 128), kind),
            pltpu.VMEM((quads, deep, 128), kind),
            pltpu.VMEM((entries * BLOCK // 128, row_total * FINE, 128), jnp.float32),
            pltpu.VMEM((all_rows * bases * 4, BLOCK, channels), kind),
            pltpu.SemaphoreType.DMA((sections, n)),
            pltpu.SemaphoreType.DMA((sections, n)),
            pltpu.SemaphoreType.DMA((sections, 2)),
            pltpu.SemaphoreType.DMA((sections, 2)),
        ],
        compiler_params=pltpu.CompilerParams(
            collective_id=0, has_side_effects=True, vmem_limit_bytes=58 * 2**20
        ),
    )(places, quadrature, latent, filters, values)


def solution(mesh):
    def chosen(latent, *rest):
        packed = latent.shape[1] % 16 == 0
        return (on_device_packed if packed else on_device)(latent, *rest)

    in_specs = (P("grp", "lon", None), P(), P(), P(), P(), P(), P(), P())
    out_specs = P("grp", "lon", None)
    return jax.shard_map(
        chosen, mesh=mesh, in_specs=in_specs, out_specs=out_specs, check_vma=False
    )
```
